1024 devices in a mesh: space: 32 (over y, x, core), freq: 32 (over z).
Axes of the slice: x: 4, y: 4, z: 32, core: 2. Of those that a mesh axis runs over, the one named last changes fastest.
Arguments:
- snapshots: bfloat16 [131072, 8192], P('space', 'freq'), may hold values from -6 to 6
- tail: bfloat16 [131072, 128], P('space'), may hold values from -6 to 6
Outputs:
- gram: float32 [128, 2, 64, 64], P('freq', None, 'space')
- spectrum: float32 [128], P('freq')
The draws below stay inside these ranges and needn't reach their ends.
All inputs are finite; a program needn't handle non-finite values.
Results may differ from the reference program's by a relative error of at most 0.0038.
Values may be sent and summed in bfloat16 or wider, within the bound.
No kernel may reach another device: no remote copies, remote signals or barrier semaphores. Data moves between devices by JAX's collectives and lax.ppermute only.
A program may use at most 64 MiB of HBM per device.

```python
import math
import jax
import jax.numpy as jnp
from jax import lax

PTS_DEV = 4096
NFFT = 256
POWER = 4
HALF = 128
POINTS = 131072
NB = 64
NF = 128
SNAPS = 8192
N_SPACE = 32


def steps_of(stream_key, dims, split, least, top_value):
    factor_of = 1.0
    for dim, shards_of in split:
        heights = jax.random.uniform(jax.random.fold_in(jax.random.fold_in(stream_key, 6), dim), (shards_of,), jnp.float32, least / len(split), top_value / len(split))
        factor_of = factor_of * jnp.repeat(jnp.exp(heights), dims[dim] // shards_of).reshape((-1,) + (1,) * (len(dims) - 1 - dim))
    return factor_of


def bell_draw(stream_key, extent, deviation, most, pieces=(), held_as=jnp.bfloat16):
    drawn = jax.random.normal(stream_key, extent, jnp.float32) * deviation
    if len(pieces) > 0:
        drawn = steps_of(stream_key, extent, pieces, -0.22, 0.18) * drawn
    return jnp.clip(drawn, min=-most, max=most).astype(held_as)


def setup_inputs(seed: int = 0) -> dict:
    seeds = jax.random.split(jax.random.key(seed), 3)
    return {
        "snapshots": bell_draw(seeds[0], (POINTS, SNAPS), 1.0, 6.0, ((0, 32), (1, 32))),
        "tail": bell_draw(seeds[1], (POINTS, HALF), 1.0, 6.0, ((0, 32),)),
    }


def build_table(count):
    steps = jnp.arange(NFFT, dtype=jnp.int32)
    freqs = jnp.arange(count, dtype=jnp.int32)
    window = 0.5 - 0.5 * jnp.cos(2.0 * math.pi * steps.astype(jnp.float32) / NFFT)
    phase = 2.0 * math.pi * (steps[:, None] * freqs[None, :] % NFFT).astype(jnp.float32) / NFFT
    table = jnp.concatenate([window[:, None] * jnp.cos(phase), -window[:, None] * jnp.sin(phase)], 1)
    return (table.astype(jnp.bfloat16), jnp.sum(window * window))

def apply_matrix(matrix, vector):
    high = lax.Precision.HIGHEST
    m_real, m_imag = (matrix[:, 0], matrix[:, 1])
    v_real, v_imag = (vector[:, 0], vector[:, 1])
    u_real = jnp.einsum('fjk,fk->fj', m_real, v_real, precision=high) - jnp.einsum('fjk,fk->fj', m_imag, v_imag, precision=high)
    u_imag = jnp.einsum('fjk,fk->fj', m_real, v_imag, precision=high) + jnp.einsum('fjk,fk->fj', m_imag, v_real, precision=high)
    return jnp.stack([u_real, u_imag], 1)

def rescale(product):
    return product / jnp.sqrt(lax.optimization_barrier(jnp.mean(product * product, axis=(1, 2), keepdims=True)) + 1e-06)

def rayleigh(vector, product):
    return lax.optimization_barrier(jnp.mean(vector * product, axis=(1, 2))) / (lax.optimization_barrier(jnp.mean(vector * vector, axis=(1, 2))) + 1e-06)

def reference(snapshots, tail):
    pressure = jnp.concatenate([snapshots, tail], 1)
    table, wsum = build_table(NF)
    table_wide = table.astype(jnp.float32)
    high = lax.Precision.HIGHEST

    def span_gram(total, index):
        rows = lax.dynamic_slice_in_dim(pressure, index * PTS_DEV, PTS_DEV, 0)
        halves = rows.reshape(PTS_DEV, NB + 1, HALF)
        blocks = jnp.concatenate([halves[:, :-1], halves[:, 1:]], 2).astype(jnp.float32)
        coef = jnp.einsum('pbt,tk->bkp', blocks, table_wide, precision=high)
        coef = coef.astype(jnp.bfloat16).astype(jnp.float32).reshape(NB, 2, NF, PTS_DEV)
        big = jnp.einsum('bcfp,gdfp->fcbdg', coef, coef, precision=high)
        return (total + big, None)
    start = jnp.zeros((NF, 2, NB, 2, NB), jnp.float32)
    big, unused = lax.scan(span_gram, start, jnp.arange(N_SPACE, dtype=jnp.int32))
    real = big[:, 0, :, 0, :] + big[:, 1, :, 1, :]
    imag = big[:, 0, :, 1, :] - big[:, 1, :, 0, :]
    gram = jnp.stack([real, imag], 1) / (POINTS * wsum)
    vector = jnp.stack([jnp.ones((NF, NB), jnp.float32), jnp.zeros((NF, NB), jnp.float32)], 1)
    for step in range(POWER):
        vector = rescale(apply_matrix(gram, vector))
    spectrum = rayleigh(vector, apply_matrix(gram, vector))
    return (gram, spectrum)
```

```python
import math

import jax
import jax.numpy as jnp
import numpy as np
from jax import lax
from jax.experimental import pallas as pl
from jax.experimental.pallas import tpu as pltpu
from jax.sharding import PartitionSpec as P

NFFT = 256
HALF = NFFT // 2
POWER = 4
BLOCKS = 64
FREQS = 128
PITCH = 2 * FREQS + 8
GROUPS = 32
NT = (((1,), (1,)), ((), ()))


def build_table():
    steps = jnp.arange(NFFT, dtype=jnp.int32)
    freqs = jnp.arange(FREQS, dtype=jnp.int32)
    window = 0.5 - 0.5 * jnp.cos(2.0 * math.pi * steps.astype(jnp.float32) / NFFT)
    phase = 2.0 * math.pi * (freqs[:, None] * steps[None, :] % NFFT).astype(jnp.float32) / NFFT
    table = jnp.concatenate(
        [window[None, :] * jnp.cos(phase), -window[None, :] * jnp.sin(phase)], 0
    )
    return (table.astype(jnp.bfloat16), jnp.sum(window * window))


def gram_kernel(factor_ref, raw_ref, tail_ref, table_ref, out_ref, coef_ref, sums_ref):
    points = raw_ref.shape[1]

    def put(block, rows):
        coef = lax.dot_general(table_ref[...], rows, NT, preferred_element_type=jnp.float32)
        start = pl.multiple_of(block * PITCH, 8)
        coef_ref[pl.ds(start, 2 * FREQS), :] = coef

    def transform(z, carry):
        rows = raw_ref[z]
        put(2 * z, rows)
        put(2 * z + 1, jnp.concatenate([rows[:, HALF:], raw_ref[z + 1][:, :HALF]], 1))
        return carry

    lax.fori_loop(0, GROUPS - 1, transform, 0, unroll=True)
    rows = raw_ref[GROUPS - 1]
    put(2 * GROUPS - 2, rows)
    put(2 * GROUPS - 1, jnp.concatenate([rows[:, HALF:], tail_ref[...]], 1))

    row = lax.broadcasted_iota(jnp.int32, (BLOCKS, 2 * BLOCKS), 0)
    lane = lax.broadcasted_iota(jnp.int32, (BLOCKS, 2 * BLOCKS), 1)
    first = ((lane < BLOCKS) & (row <= lane)) | ((lane >= BLOCKS) & (row > lane - BLOCKS))

    def product(f, swap):
        real = coef_ref[pl.ds(f, BLOCKS, stride=PITCH), :].astype(jnp.bfloat16)
        imag = coef_ref[pl.ds(FREQS + f, BLOCKS, stride=PITCH), :].astype(jnp.bfloat16)
        left = jnp.concatenate([real, imag], 1)
        turned = jnp.concatenate([imag, -real], 1)
        right = jnp.concatenate([turned, left] if swap else [left, turned], 0)
        return lax.dot_general(left, right, NT, preferred_element_type=jnp.float32)

    def packed(f):
        return jnp.where(first, product(f, False), product(f + 1, True))

    def gram(step, carry):
        base = 8 * step
        for core in range(2):
            upper = packed(base + 2 * core)
            lower = packed(base + 4 + 2 * core)
            for chip in range(GROUPS // 2):
                part = slice(4 * chip, 4 * chip + 4)
                start = pl.multiple_of(base, 8)
                sums_ref[2 * chip + core, pl.ds(start, 8), :] = jnp.concatenate(
                    [upper[part], lower[part]], 0
                )
        return carry

    lax.fori_loop(0, FREQS // 8, gram, 0, unroll=2)
    factor = factor_ref[0]
    for index in range(GROUPS):
        out_ref[index] = (sums_ref[index] * factor).astype(jnp.bfloat16)


def gram_call(factor, raw, tail, table):
    points = raw.shape[1]
    return pl.pallas_call(
        gram_kernel,
        out_shape=jax.ShapeDtypeStruct((GROUPS, FREQS, 2 * BLOCKS), jnp.bfloat16),
        in_specs=[
            pl.BlockSpec(memory_space=pltpu.SMEM),
            pl.BlockSpec(memory_space=pltpu.VMEM),
            pl.BlockSpec(memory_space=pltpu.VMEM),
            pl.BlockSpec(memory_space=pltpu.VMEM),
        ],
        out_specs=pl.BlockSpec(memory_space=pltpu.VMEM),
        scratch_shapes=[
            pltpu.VMEM((BLOCKS * PITCH, points), jnp.float32),
            pltpu.VMEM((GROUPS, FREQS, 2 * BLOCKS), jnp.float32),
        ],
        compiler_params=pltpu.CompilerParams(vmem_limit_bytes=40 * 1024 * 1024),
        name="gram",
    )(factor, raw, tail, table)


def power_kernel(place_ref, scale_ref, sums_ref, rows_ref, spectrum_ref, matrix_ref):
    scale = scale_ref[0]
    row = lax.broadcasted_iota(jnp.int32, (BLOCKS, BLOCKS), 0)
    column = lax.broadcasted_iota(jnp.int32, (BLOCKS, BLOCKS), 1)
    matrices = []
    for core in range(2):
        held = jnp.concatenate([sums_ref[2 * c + core] for c in range(GROUPS // 2)], 0) * scale
        left, right = (held[:, :BLOCKS], held[:, BLOCKS:])
        left_t, right_t = (left.T, right.T)
        real_even = jnp.where(row <= column, left, left_t)
        real_odd = jnp.where(row <= column, right, right_t)
        zero = jnp.zeros_like(left)
        imag_odd = jnp.where(row > column, left, jnp.where(row < column, -left_t, zero))
        imag_even = jnp.where(row > column, right, jnp.where(row < column, -right_t, zero))
        matrices.append(jnp.concatenate([real_even, imag_even], 1))
        matrices.append(jnp.concatenate([real_odd, imag_odd], 1))
    matrix = jnp.stack(matrices, 0)
    matrix_ref[...] = matrix
    place = place_ref[0]
    for k in range(2):
        rows_ref[:, k : k + 1, :] = matrix_ref[:, pl.ds(2 * place + k, 1), :]

    low = lax.broadcasted_iota(jnp.int32, (4, 1, 2 * BLOCKS), 2) < BLOCKS
    count = 2.0 * BLOCKS

    def turn(v):
        return jnp.concatenate([v[:, :, BLOCKS:], v[:, :, :BLOCKS]], 2)

    def from_columns(v_real, v_imag):
        a = jnp.sum(matrix * v_real, axis=1, keepdims=True)
        b = jnp.sum(matrix * v_imag, axis=1, keepdims=True)
        return jnp.where(low, a, -a) + turn(b)

    def from_rows(v):
        u_real = jnp.sum(matrix * jnp.where(low, v, -v), axis=2, keepdims=True)
        u_imag = jnp.sum(matrix * turn(v), axis=2, keepdims=True)
        return (u_real, u_imag)

    def scaled_columns(u_real, u_imag):
        m = jnp.sum(u_real * u_real + u_imag * u_imag, axis=1, keepdims=True) / count
        norm = jnp.sqrt(m + 1e-06)
        return (u_real / norm, u_imag / norm)

    def scaled_rows(u):
        return u / jnp.sqrt(jnp.sum(u * u, axis=2, keepdims=True) / count + 1e-06)

    v = jnp.where(low, jnp.ones((4, 1, 2 * BLOCKS), jnp.float32), 0.0)
    for step in range(POWER // 2):
        v = scaled_rows(from_columns(*scaled_columns(*from_rows(v))))
    u_real, u_imag = from_rows(v)
    lane = lax.broadcasted_iota(jnp.int32, (4, BLOCKS, 2 * BLOCKS), 2)
    line = lax.broadcasted_iota(jnp.int32, (4, BLOCKS, 2 * BLOCKS), 1)
    v_real = jnp.sum(jnp.where(lane == line, v, 0.0), axis=2, keepdims=True)
    v_imag = jnp.sum(jnp.where(lane == line + BLOCKS, v, 0.0), axis=2, keepdims=True)
    top = jnp.sum(v_real * u_real + v_imag * u_imag, axis=1, keepdims=True) / count
    below = jnp.sum(v_real * v_real + v_imag * v_imag, axis=1, keepdims=True) / count
    spectrum_ref[...] = jnp.broadcast_to(top / (below + 1e-06), spectrum_ref.shape)


def power_call(place, scale, sums):
    return pl.pallas_call(
        power_kernel,
        out_shape=(
            jax.ShapeDtypeStruct((4, 2, 2 * BLOCKS), jnp.float32),
            jax.ShapeDtypeStruct((4, 1, 2 * BLOCKS), jnp.float32),
        ),
        in_specs=[
            pl.BlockSpec(memory_space=pltpu.SMEM),
            pl.BlockSpec(memory_space=pltpu.SMEM),
            pl.BlockSpec(memory_space=pltpu.VMEM),
        ],
        out_specs=(
            pl.BlockSpec(memory_space=pltpu.VMEM),
            pl.BlockSpec(memory_space=pltpu.VMEM),
        ),
        scratch_shapes=[pltpu.VMEM((4, BLOCKS, 2 * BLOCKS), jnp.float32)],
        compiler_params=pltpu.CompilerParams(vmem_limit_bytes=16 * 1024 * 1024),
        name="power",
    )(place, scale, sums)


def shards(snapshots, tail):
    points = snapshots.shape[0]
    space = lax.axis_index("space")
    freq = lax.axis_index("freq")
    each = points // GROUPS
    table, wsum = build_table()
    scale = 1.0 / (points * GROUPS * wsum)
    raw = lax.all_to_all(snapshots.reshape(GROUPS, each, NFFT), "freq", 0, 0)
    own_tail = lax.dynamic_slice_in_dim(tail, freq * each, each, 0)
    factors = np.exp2(np.arange(GROUPS) / GROUPS).astype(np.float32)
    factor = jnp.exp2(space.astype(jnp.float32) / GROUPS)
    sums = gram_call(factor.reshape(1), raw, own_tail, table)
    parts = lax.all_to_all(sums, "space", 0, 0)
    undo = jnp.asarray(1.0 / factors, jnp.float32)[:, None, None]
    mine = jnp.sum(parts.astype(jnp.float32) * undo, 0).reshape(GROUPS, 4, 2 * BLOCKS)
    mine = jnp.sum(lax.all_to_all(mine, "freq", 0, 0), 0)
    whole = lax.all_to_all(jnp.broadcast_to(mine[None], (GROUPS,) + mine.shape), "space", 0, 0)
    rows, spectrum = power_call(space.reshape(1), scale.reshape(1), whole)
    return (rows.reshape(4, 2, 2, BLOCKS).transpose(0, 2, 1, 3), spectrum[:, 0, 0])


def solution(mesh):
    in_specs = (P("space", "freq"), P("space", None))
    out_specs = (P("freq", None, "space", None), P("freq"))
    return jax.shard_map(shards, mesh=mesh, in_specs=in_specs, out_specs=out_specs, check_vma=False)
```

```python
import functools
import math

import jax
import jax.numpy as jnp
import numpy as np
from jax import lax
from jax.experimental import pallas as pl
from jax.experimental.pallas import tpu as pltpu
from jax.sharding import PartitionSpec as P

NFFT = 256
HALF = NFFT // 2
POWER = 4
BLOCKS = 64
FREQS = 128
PITCH = 2 * FREQS + 8
GROUPS = 32
CHIPS = GROUPS // 2
NT = (((1,), (1,)), ((), ()))


def build_table():
    steps = jnp.arange(NFFT, dtype=jnp.int32)
    freqs = jnp.arange(FREQS, dtype=jnp.int32)
    window = 0.5 - 0.5 * jnp.cos(2.0 * math.pi * steps.astype(jnp.float32) / NFFT)
    phase = 2.0 * math.pi * (freqs[:, None] * steps[None, :] % NFFT).astype(jnp.float32) / NFFT
    table = jnp.concatenate(
        [window[None, :] * jnp.cos(phase), -window[None, :] * jnp.sin(phase)], 0
    )
    return table.astype(jnp.bfloat16)


def gram_kernel(core_ref, raw_ref, tail_ref, table_ref, out_ref, coef_ref):
    def put(block, rows):
        coef = lax.dot_general(table_ref[...], rows, NT, preferred_element_type=jnp.float32)
        start = pl.multiple_of(block * PITCH, 8)
        coef_ref[pl.ds(start, 2 * FREQS), :] = coef

    def transform(z, carry):
        rows = raw_ref[z]
        put(2 * z, rows)
        put(2 * z + 1, jnp.concatenate([rows[:, HALF:], raw_ref[z + 1][:, :HALF]], 1))
        return carry

    lax.fori_loop(0, GROUPS - 1, transform, 0, unroll=True)
    rows = raw_ref[GROUPS - 1]
    put(2 * GROUPS - 2, rows)
    put(2 * GROUPS - 1, jnp.concatenate([rows[:, HALF:], tail_ref[...]], 1))

    row = lax.broadcasted_iota(jnp.int32, (BLOCKS, 2 * BLOCKS), 0)
    lane = lax.broadcasted_iota(jnp.int32, (BLOCKS, 2 * BLOCKS), 1)
    first = ((lane < BLOCKS) & (row <= lane)) | ((lane >= BLOCKS) & (row > lane - BLOCKS))

    def product(f, swap):
        real = coef_ref[pl.ds(f, BLOCKS, stride=PITCH), :].astype(jnp.bfloat16)
        imag = coef_ref[pl.ds(FREQS + f, BLOCKS, stride=PITCH), :].astype(jnp.bfloat16)
        left = jnp.concatenate([real, imag], 1)
        turned = jnp.concatenate([imag, -real], 1)
        right = jnp.concatenate([turned, left] if swap else [left, turned], 0)
        return lax.dot_general(left, right, NT, preferred_element_type=jnp.float32)

    def packed(f):
        return jnp.where(first, product(f, False), product(f + 1, True))

    core = core_ref[0]

    def gram(step, carry):
        base = 8 * step
        upper = packed(base + 2 * core)
        lower = packed(base + 4 + 2 * core)
        start = pl.multiple_of(base, 8)
        for chip in range(CHIPS):
            part = slice(4 * chip, 4 * chip + 4)
            out_ref[chip, pl.ds(start, 8), :] = jnp.concatenate([upper[part], lower[part]], 0)
        return carry

    lax.fori_loop(0, FREQS // 8, gram, 0, unroll=4)


def gram_call(core, raw, tail, table):
    points = raw.shape[1]
    return pl.pallas_call(
        gram_kernel,
        out_shape=jax.ShapeDtypeStruct((CHIPS, FREQS, 2 * BLOCKS), jnp.float32),
        in_specs=[
            pl.BlockSpec(memory_space=pltpu.SMEM),
            pl.BlockSpec(memory_space=pltpu.VMEM),
            pl.BlockSpec(memory_space=pltpu.VMEM),
            pl.BlockSpec(memory_space=pltpu.VMEM),
        ],
        out_specs=pl.BlockSpec(memory_space=pltpu.VMEM),
        scratch_shapes=[pltpu.VMEM((BLOCKS * PITCH, points), jnp.float32)],
        compiler_params=pltpu.CompilerParams(vmem_limit_bytes=40 * 1024 * 1024),
        name="gram",
    )(core.reshape(1), raw, tail, table)


def power_kernel(scale, place_ref, sums_ref, rows_ref, spectrum_ref, matrix_ref):
    row = lax.broadcasted_iota(jnp.int32, (BLOCKS, BLOCKS), 0)
    column = lax.broadcasted_iota(jnp.int32, (BLOCKS, BLOCKS), 1)
    matrices = []
    for core in range(2):
        held = jnp.concatenate([sums_ref[2 * c + core] for c in range(CHIPS)], 0) * scale
        left, right = (held[:, :BLOCKS], held[:, BLOCKS:])
        left_t, right_t = (left.T, right.T)
        real_even = jnp.where(row <= column, left, left_t)
        real_odd = jnp.where(row <= column, right, right_t)
        zero = jnp.zeros_like(left)
        imag_odd = jnp.where(row > column, left, jnp.where(row < column, -left_t, zero))
        imag_even = jnp.where(row > column, right, jnp.where(row < column, -right_t, zero))
        matrices.append(jnp.concatenate([real_even, imag_even], 1))
        matrices.append(jnp.concatenate([real_odd, imag_odd], 1))
    matrix = jnp.stack(matrices, 0)
    matrix_ref[...] = matrix
    place = place_ref[0]
    for k in range(2):
        line = matrix_ref[:, pl.ds(2 * place + k, 1), :]
        rows_ref[:, 0, k : k + 1, :] = line[:, :, :BLOCKS]
        rows_ref[:, 1, k : k + 1, :] = line[:, :, BLOCKS:]

    low = lax.broadcasted_iota(jnp.int32, (4, 1, 2 * BLOCKS), 2) < BLOCKS
    count = 2.0 * BLOCKS

    def turn(v):
        return jnp.concatenate([v[:, :, BLOCKS:], v[:, :, :BLOCKS]], 2)

    def from_columns(v_real, v_imag):
        a = jnp.sum(matrix * v_real, axis=1, keepdims=True)
        b = jnp.sum(matrix * v_imag, axis=1, keepdims=True)
        return jnp.where(low, a, -a) + turn(b)

    def from_rows(v):
        u_real = jnp.sum(matrix * jnp.where(low, v, -v), axis=2, keepdims=True)
        u_imag = jnp.sum(matrix * turn(v), axis=2, keepdims=True)
        return (u_real, u_imag)

    def scaled_columns(u_real, u_imag):
        m = jnp.sum(u_real * u_real + u_imag * u_imag, axis=1, keepdims=True) / count
        norm = jnp.sqrt(m + 1e-06)
        return (u_real / norm, u_imag / norm)

    def scaled_rows(u):
        return u / jnp.sqrt(jnp.sum(u * u, axis=2, keepdims=True) / count + 1e-06)

    v = jnp.where(low, jnp.ones((4, 1, 2 * BLOCKS), jnp.float32), 0.0)
    for step in range(POWER // 2):
        v = scaled_rows(from_columns(*scaled_columns(*from_rows(v))))
    u_real, u_imag = from_rows(v)
    lane = lax.broadcasted_iota(jnp.int32, (4, BLOCKS, 2 * BLOCKS), 2)
    line = lax.broadcasted_iota(jnp.int32, (4, BLOCKS, 2 * BLOCKS), 1)
    v_real = jnp.sum(jnp.where(lane == line, v, 0.0), axis=2, keepdims=True)
    v_imag = jnp.sum(jnp.where(lane == line + BLOCKS, v, 0.0), axis=2, keepdims=True)
    top = jnp.sum(v_real * u_real + v_imag * u_imag, axis=1, keepdims=True) / count
    below = jnp.sum(v_real * v_real + v_imag * v_imag, axis=1, keepdims=True) / count
    ratio = top / (below + 1e-06)
    for f in range(4):
        spectrum_ref[f] = ratio[f, 0, 0]


def power_call(place, scale, sums):
    return pl.pallas_call(
        functools.partial(power_kernel, scale),
        out_shape=(
            jax.ShapeDtypeStruct((4, 2, 2, BLOCKS), jnp.float32),
            jax.ShapeDtypeStruct((4,), jnp.float32),
        ),
        in_specs=[
            pl.BlockSpec(memory_space=pltpu.SMEM),
            pl.BlockSpec(memory_space=pltpu.VMEM),
        ],
        out_specs=(
            pl.BlockSpec(memory_space=pltpu.VMEM),
            pl.BlockSpec(memory_space=pltpu.SMEM),
        ),
        scratch_shapes=[pltpu.VMEM((4, BLOCKS, 2 * BLOCKS), jnp.float32)],
        compiler_params=pltpu.CompilerParams(vmem_limit_bytes=16 * 1024 * 1024),
        name="power",
    )(place.reshape(1), sums)


def shards(snapshots, tail):
    points = snapshots.shape[0]
    space = lax.axis_index("space")
    freq = lax.axis_index("freq")
    each = points // GROUPS
    table = build_table()
    scale = 1.0 / (points * GROUPS * (0.375 * NFFT))
    raw = lax.all_to_all(snapshots.reshape(GROUPS, each, NFFT), "freq", 0, 0)
    own_tail = lax.dynamic_slice_in_dim(tail, freq * each, each, 0)
    core = space % 2
    chip = space // 2
    other = gram_call(1 - core, raw, own_tail, table)
    other = lax.ppermute(other, "space", [(s, s ^ 1) for s in range(GROUPS)])
    sums = gram_call(core, raw, own_tail, table) + other
    factor = jnp.exp2(chip.astype(jnp.float32) / CHIPS)
    undo = jnp.asarray(np.exp2(-np.arange(CHIPS) / CHIPS), jnp.float32)[:, None, None]
    parts = lax.all_to_all(
        (sums * factor).astype(jnp.bfloat16),
        "space",
        0,
        0,
        axis_index_groups=[[2 * i + c for i in range(CHIPS)] for c in range(2)],
    )
    mine = jnp.sum(parts.astype(jnp.float32) * undo, 0).reshape(GROUPS, 4, 2 * BLOCKS)
    mine = jnp.sum(lax.all_to_all(mine, "freq", 0, 0), 0)
    whole = lax.all_to_all(jnp.broadcast_to(mine[None], (GROUPS,) + mine.shape), "space", 0, 0)
    return power_call(space, scale, whole)


def solution(mesh):
    in_specs = (P("space", "freq"), P("space", None))
    out_specs = (P("freq", None, "space", None), P("freq"))
    return jax.shard_map(shards, mesh=mesh, in_specs=in_specs, out_specs=out_specs, check_vma=False)
```

```python
import functools
import math

import jax
import jax.numpy as jnp
import numpy as np
from jax import lax
from jax.experimental import pallas as pl
from jax.experimental.pallas import tpu as pltpu
from jax.sharding import PartitionSpec as P

NFFT = 256
HALF = NFFT // 2
POWER = 4
BLOCKS = 64
FREQS = 128
PITCH = 2 * FREQS + 8
GROUPS = 32
CHIPS = GROUPS // 2
ORDER = [int(format(r, "05b")[::-1], 2) for r in range(GROUPS)]
RANK = [ORDER.index(z) for z in range(GROUPS)]
NT = (((1,), (1,)), ((), ()))


def build_table():
    steps = jnp.arange(NFFT, dtype=jnp.int32)
    freqs = jnp.arange(FREQS, dtype=jnp.int32)
    window = 0.5 - 0.5 * jnp.cos(2.0 * math.pi * steps.astype(jnp.float32) / NFFT)
    phase = 2.0 * math.pi * (freqs[:, None] * steps[None, :] % NFFT).astype(jnp.float32) / NFFT
    table = jnp.concatenate(
        [window[None, :] * jnp.cos(phase), -window[None, :] * jnp.sin(phase)], 0
    )
    return table.astype(jnp.bfloat16)


def gram_kernel(core_ref, raw_ref, tail_ref, table_ref, out_ref, coef_ref):
    def put(block, rows):
        coef = lax.dot_general(table_ref[...], rows, NT, preferred_element_type=jnp.float32)
        coef_ref[pl.ds(block * PITCH, 2 * FREQS), :] = coef

    for z in range(GROUPS):
        rows = raw_ref[RANK[z]]
        after = tail_ref[...] if z == GROUPS - 1 else raw_ref[RANK[z + 1]][:, :HALF]
        put(2 * z, rows)
        put(2 * z + 1, jnp.concatenate([rows[:, HALF:], after], 1))

    row = lax.broadcasted_iota(jnp.int32, (BLOCKS, 2 * BLOCKS), 0)
    lane = lax.broadcasted_iota(jnp.int32, (BLOCKS, 2 * BLOCKS), 1)
    first = ((lane < BLOCKS) & (row <= lane)) | ((lane >= BLOCKS) & (row > lane - BLOCKS))

    def product(f, swap):
        real = coef_ref[pl.ds(f, BLOCKS, stride=PITCH), :].astype(jnp.bfloat16)
        imag = coef_ref[pl.ds(FREQS + f, BLOCKS, stride=PITCH), :].astype(jnp.bfloat16)
        left = jnp.concatenate([real, imag], 1)
        turned = jnp.concatenate([imag, -real], 1)
        right = jnp.concatenate([turned, left] if swap else [left, turned], 0)
        return lax.dot_general(left, right, NT, preferred_element_type=jnp.float32)

    def packed(f):
        return jnp.where(first, product(f, False), product(f + 1, True))

    core = core_ref[0]

    def gram(step, carry):
        base = 8 * step
        upper = packed(base + 2 * core)
        lower = packed(base + 4 + 2 * core)
        start = pl.multiple_of(base, 8)
        for chip in range(CHIPS):
            part = slice(4 * chip, 4 * chip + 4)
            out_ref[chip, pl.ds(start, 8), :] = jnp.concatenate([upper[part], lower[part]], 0)
        return carry

    lax.fori_loop(0, FREQS // 8, gram, 0, unroll=4)


def gram_call(core, raw, tail, table):
    points = raw.shape[1]
    return pl.pallas_call(
        gram_kernel,
        out_shape=jax.ShapeDtypeStruct((CHIPS, FREQS, 2 * BLOCKS), jnp.float32),
        in_specs=[
            pl.BlockSpec(memory_space=pltpu.SMEM),
            pl.BlockSpec(memory_space=pltpu.VMEM),
            pl.BlockSpec(memory_space=pltpu.VMEM),
            pl.BlockSpec(memory_space=pltpu.VMEM),
        ],
        out_specs=pl.BlockSpec(memory_space=pltpu.VMEM),
        scratch_shapes=[pltpu.VMEM((BLOCKS * PITCH, points), jnp.float32)],
        compiler_params=pltpu.CompilerParams(vmem_limit_bytes=16 * 1024 * 1024),
        name="gram",
    )(core.reshape(1), raw, tail, table)


def power_kernel(scale, place_ref, sums_ref, rows_ref, spectrum_ref, matrix_ref):
    row = lax.broadcasted_iota(jnp.int32, (BLOCKS, BLOCKS), 0)
    column = lax.broadcasted_iota(jnp.int32, (BLOCKS, BLOCKS), 1)
    matrices = []
    for core in range(2):
        held = jnp.concatenate([sums_ref[2 * c + core] for c in range(CHIPS)], 0) * scale
        left, right = (held[:, :BLOCKS], held[:, BLOCKS:])
        left_t, right_t = (left.T, right.T)
        real_even = jnp.where(row <= column, left, left_t)
        real_odd = jnp.where(row <= column, right, right_t)
        zero = jnp.zeros_like(left)
        imag_odd = jnp.where(row > column, left, jnp.where(row < column, -left_t, zero))
        imag_even = jnp.where(row > column, right, jnp.where(row < column, -right_t, zero))
        matrices.append(jnp.concatenate([real_even, imag_even], 1))
        matrices.append(jnp.concatenate([real_odd, imag_odd], 1))
    matrix = jnp.stack(matrices, 0)
    matrix_ref[...] = matrix
    place = place_ref[0]
    for k in range(2):
        line = matrix_ref[:, pl.ds(2 * place + k, 1), :]
        rows_ref[:, 0, k : k + 1, :] = line[:, :, :BLOCKS]
        rows_ref[:, 1, k : k + 1, :] = line[:, :, BLOCKS:]

    low = lax.broadcasted_iota(jnp.int32, (4, 1, 2 * BLOCKS), 2) < BLOCKS
    count = 2.0 * BLOCKS

    def turn(v):
        return jnp.concatenate([v[:, :, BLOCKS:], v[:, :, :BLOCKS]], 2)

    def from_columns(v_real, v_imag):
        a = jnp.sum(matrix * v_real, axis=1, keepdims=True)
        b = jnp.sum(matrix * v_imag, axis=1, keepdims=True)
        return jnp.where(low, a, -a) + turn(b)

    def from_rows(v):
        u_real = jnp.sum(matrix * jnp.where(low, v, -v), axis=2, keepdims=True)
        u_imag = jnp.sum(matrix * turn(v), axis=2, keepdims=True)
        return (u_real, u_imag)

    def scaled_columns(u_real, u_imag):
        m = jnp.sum(u_real * u_real + u_imag * u_imag, axis=1, keepdims=True) / count
        norm = jnp.sqrt(m + 1e-06)
        return (u_real / norm, u_imag / norm)

    def scaled_rows(u):
        return u / jnp.sqrt(jnp.sum(u * u, axis=2, keepdims=True) / count + 1e-06)

    v = jnp.where(low, jnp.ones((4, 1, 2 * BLOCKS), jnp.float32), 0.0)
    for step in range(POWER // 2):
        v = scaled_rows(from_columns(*scaled_columns(*from_rows(v))))
    u_real, u_imag = from_rows(v)
    lane = lax.broadcasted_iota(jnp.int32, (4, BLOCKS, 2 * BLOCKS), 2)
    line = lax.broadcasted_iota(jnp.int32, (4, BLOCKS, 2 * BLOCKS), 1)
    v_real = jnp.sum(jnp.where(lane == line, v, 0.0), axis=2, keepdims=True)
    v_imag = jnp.sum(jnp.where(lane == line + BLOCKS, v, 0.0), axis=2, keepdims=True)
    top = jnp.sum(v_real * u_real + v_imag * u_imag, axis=1, keepdims=True) / count
    below = jnp.sum(v_real * v_real + v_imag * v_imag, axis=1, keepdims=True) / count
    ratio = top / (below + 1e-06)
    for f in range(4):
        spectrum_ref[f] = ratio[f, 0, 0]


def power_call(place, scale, sums):
    return pl.pallas_call(
        functools.partial(power_kernel, scale),
        out_shape=(
            jax.ShapeDtypeStruct((4, 2, 2, BLOCKS), jnp.float32),
            jax.ShapeDtypeStruct((4,), jnp.float32),
        ),
        in_specs=[
            pl.BlockSpec(memory_space=pltpu.SMEM),
            pl.BlockSpec(memory_space=pltpu.VMEM),
        ],
        out_specs=(
            pl.BlockSpec(memory_space=pltpu.VMEM),
            pl.BlockSpec(memory_space=pltpu.SMEM),
        ),
        scratch_shapes=[pltpu.VMEM((4, BLOCKS, 2 * BLOCKS), jnp.float32)],
        compiler_params=pltpu.CompilerParams(vmem_limit_bytes=16 * 1024 * 1024),
        name="power",
    )(place.reshape(1), sums)


def shards(snapshots, tail):
    points = snapshots.shape[0]
    space = lax.axis_index("space")
    freq = lax.axis_index("freq")
    each = points // GROUPS
    table = build_table()
    scale = 1.0 / (points * GROUPS * (0.375 * NFFT))
    raw = lax.all_to_all(
        snapshots.reshape(GROUPS, each, NFFT), "freq", 0, 0, axis_index_groups=[ORDER]
    )
    rank = sum(((freq >> bit) & 1) << (4 - bit) for bit in range(5))
    own_tail = lax.dynamic_slice_in_dim(tail, rank * each, each, 0)
    core = space % 2
    chip = space // 2
    other = gram_call(1 - core, raw, own_tail, table)
    other = lax.ppermute(other, "space", [(s, s ^ 1) for s in range(GROUPS)])
    sums = gram_call(core, raw, own_tail, table) + other
    factor = jnp.exp2(chip.astype(jnp.float32) / CHIPS)
    undo = jnp.asarray(np.exp2(-np.arange(CHIPS) / CHIPS), jnp.float32)[:, None, None]
    parts = lax.all_to_all(
        (sums * factor).astype(jnp.bfloat16),
        "space",
        0,
        0,
        axis_index_groups=[[2 * i + c for i in range(CHIPS)] for c in range(2)],
    )
    mine = jnp.sum(parts.astype(jnp.float32) * undo, 0).reshape(GROUPS, 4, 2 * BLOCKS)
    mine = jnp.sum(lax.all_to_all(mine, "freq", 0, 0), 0)
    whole = lax.all_to_all(jnp.broadcast_to(mine[None], (GROUPS,) + mine.shape), "space", 0, 0)
    return power_call(space, scale, whole)


def solution(mesh):
    in_specs = (P("space", "freq"), P("space", None))
    out_specs = (P("freq", None, "space", None), P("freq"))
    return jax.shard_map(shards, mesh=mesh, in_specs=in_specs, out_specs=out_specs, check_vma=False)
```

```python
import functools
import math

import jax
import jax.numpy as jnp
import numpy as np
from jax import lax
from jax.experimental import pallas as pl
from jax.experimental.pallas import tpu as pltpu
from jax.sharding import PartitionSpec as P

NFFT = 256
HALF = NFFT // 2
POWER = 4
BLOCKS = 64
FREQS = 128
PITCH = 2 * FREQS + 8
GROUPS = 32
CHIPS = GROUPS // 2
NT = (((1,), (1,)), ((), ()))


def build_table():
    steps = jnp.arange(NFFT, dtype=jnp.int32)
    freqs = jnp.arange(FREQS, dtype=jnp.int32)
    window = 0.5 - 0.5 * jnp.cos(2.0 * math.pi * steps.astype(jnp.float32) / NFFT)
    phase = 2.0 * math.pi * (freqs[:, None] * steps[None, :] % NFFT).astype(jnp.float32) / NFFT
    table = jnp.concatenate(
        [window[None, :] * jnp.cos(phase), -window[None, :] * jnp.sin(phase)], 0
    )
    return table.astype(jnp.bfloat16)


def gram_kernel(unroll, core_ref, factor_ref, raw_ref, tail_ref, table_ref, own_ref, other_ref, coef_ref, held_ref):
    def put(block, rows):
        coef = lax.dot_general(table_ref[...], rows, NT, preferred_element_type=jnp.float32)
        coef_ref[pl.ds(block * PITCH, 2 * FREQS), :] = coef

    for z in range(GROUPS):
        rows = raw_ref[z]
        after = tail_ref[...] if z == GROUPS - 1 else raw_ref[z + 1][:, :HALF]
        put(2 * z, rows)
        put(2 * z + 1, jnp.concatenate([rows[:, HALF:], after], 1))

    row = lax.broadcasted_iota(jnp.int32, (BLOCKS, 2 * BLOCKS), 0)
    lane = lax.broadcasted_iota(jnp.int32, (BLOCKS, 2 * BLOCKS), 1)
    first = ((lane < BLOCKS) & (row <= lane)) | ((lane >= BLOCKS) & (row > lane - BLOCKS))

    def product(f, swap):
        real = coef_ref[pl.ds(f, BLOCKS, stride=PITCH), :].astype(jnp.bfloat16)
        imag = coef_ref[pl.ds(FREQS + f, BLOCKS, stride=PITCH), :].astype(jnp.bfloat16)
        left = jnp.concatenate([real, imag], 1)
        turned = jnp.concatenate([imag, -real], 1)
        right = jnp.concatenate([turned, left] if swap else [left, turned], 0)
        return lax.dot_general(left, right, NT, preferred_element_type=jnp.float32)

    def packed(f):
        return jnp.where(first, product(f, False), product(f + 1, True))

    core = core_ref[0]

    def half(target_ref, core):
        def gram(step, carry):
            base = 8 * step
            upper = packed(base + 2 * core)
            lower = packed(base + 4 + 2 * core)
            start = pl.multiple_of(base, 8)
            for chip in range(CHIPS):
                part = slice(4 * chip, 4 * chip + 4)
                target_ref[chip, pl.ds(start, 8), :] = jnp.concatenate(
                    [upper[part], lower[part]], 0
                )
            return carry

        lax.fori_loop(0, FREQS // 8, gram, 0, unroll=unroll)

    half(held_ref, 1 - core)
    other_ref[...] = (held_ref[...] * factor_ref[0]).astype(jnp.bfloat16)
    half(own_ref, core)


def gram_call(core, factor, raw, tail, table, unroll=16):
    points = raw.shape[1]
    shape = (CHIPS, FREQS, 2 * BLOCKS)
    return pl.pallas_call(
        functools.partial(gram_kernel, unroll),
        out_shape=(
            jax.ShapeDtypeStruct(shape, jnp.float32),
            jax.ShapeDtypeStruct(shape, jnp.bfloat16),
        ),
        in_specs=[
            pl.BlockSpec(memory_space=pltpu.SMEM),
            pl.BlockSpec(memory_space=pltpu.SMEM),
            pl.BlockSpec(memory_space=pltpu.VMEM),
            pl.BlockSpec(memory_space=pltpu.VMEM),
            pl.BlockSpec(memory_space=pltpu.VMEM),
        ],
        out_specs=(
            pl.BlockSpec(memory_space=pltpu.VMEM),
            pl.BlockSpec(memory_space=pltpu.VMEM),
        ),
        scratch_shapes=[
            pltpu.VMEM((BLOCKS * PITCH, points), jnp.float32),
            pltpu.VMEM(shape, jnp.float32),
        ],
        compiler_params=pltpu.CompilerParams(vmem_limit_bytes=20 * 1024 * 1024),
        name="gram",
    )(core.reshape(1), factor.reshape(1), raw, tail, table)


def power_kernel(scale, place_ref, sums_ref, rows_ref, spectrum_ref, matrix_ref):
    row = lax.broadcasted_iota(jnp.int32, (BLOCKS, BLOCKS), 0)
    column = lax.broadcasted_iota(jnp.int32, (BLOCKS, BLOCKS), 1)
    matrices = []
    for core in range(2):
        held = jnp.concatenate([sums_ref[2 * c + core] for c in range(CHIPS)], 0) * scale
        left, right = (held[:, :BLOCKS], held[:, BLOCKS:])
        left_t, right_t = (left.T, right.T)
        real_even = jnp.where(row <= column, left, left_t)
        real_odd = jnp.where(row <= column, right, right_t)
        zero = jnp.zeros_like(left)
        imag_odd = jnp.where(row > column, left, jnp.where(row < column, -left_t, zero))
        imag_even = jnp.where(row > column, right, jnp.where(row < column, -right_t, zero))
        matrices.append(jnp.concatenate([real_even, imag_even], 1))
        matrices.append(jnp.concatenate([real_odd, imag_odd], 1))
    matrix = jnp.stack(matrices, 0)
    matrix_ref[...] = matrix
    place = place_ref[0]
    for k in range(2):
        line = matrix_ref[:, pl.ds(2 * place + k, 1), :]
        rows_ref[:, 0, k : k + 1, :] = line[:, :, :BLOCKS]
        rows_ref[:, 1, k : k + 1, :] = line[:, :, BLOCKS:]

    low = lax.broadcasted_iota(jnp.int32, (4, 1, 2 * BLOCKS), 2) < BLOCKS
    count = 2.0 * BLOCKS

    def turn(v):
        return jnp.concatenate([v[:, :, BLOCKS:], v[:, :, :BLOCKS]], 2)

    def from_columns(v_real, v_imag):
        a = jnp.sum(matrix * v_real, axis=1, keepdims=True)
        b = jnp.sum(matrix * v_imag, axis=1, keepdims=True)
        return jnp.where(low, a, -a) + turn(b)

    def from_rows(v):
        u_real = jnp.sum(matrix * jnp.where(low, v, -v), axis=2, keepdims=True)
        u_imag = jnp.sum(matrix * turn(v), axis=2, keepdims=True)
        return (u_real, u_imag)

    def scaled_columns(u_real, u_imag):
        m = jnp.sum(u_real * u_real + u_imag * u_imag, axis=1, keepdims=True) / count
        norm = jnp.sqrt(m + 1e-06)
        return (u_real / norm, u_imag / norm)

    def scaled_rows(u):
        return u / jnp.sqrt(jnp.sum(u * u, axis=2, keepdims=True) / count + 1e-06)

    v = jnp.where(low, jnp.ones((4, 1, 2 * BLOCKS), jnp.float32), 0.0)
    for step in range(POWER // 2):
        v = scaled_rows(from_columns(*scaled_columns(*from_rows(v))))
    u_real, u_imag = from_rows(v)
    lane = lax.broadcasted_iota(jnp.int32, (4, BLOCKS, 2 * BLOCKS), 2)
    line = lax.broadcasted_iota(jnp.int32, (4, BLOCKS, 2 * BLOCKS), 1)
    v_real = jnp.sum(jnp.where(lane == line, v, 0.0), axis=2, keepdims=True)
    v_imag = jnp.sum(jnp.where(lane == line + BLOCKS, v, 0.0), axis=2, keepdims=True)
    top = jnp.sum(v_real * u_real + v_imag * u_imag, axis=1, keepdims=True) / count
    below = jnp.sum(v_real * v_real + v_imag * v_imag, axis=1, keepdims=True) / count
    ratio = top / (below + 1e-06)
    for f in range(4):
        spectrum_ref[f] = ratio[f, 0, 0]


def power_call(place, scale, sums):
    return pl.pallas_call(
        functools.partial(power_kernel, scale),
        out_shape=(
            jax.ShapeDtypeStruct((4, 2, 2, BLOCKS), jnp.float32),
            jax.ShapeDtypeStruct((4,), jnp.float32),
        ),
        in_specs=[
            pl.BlockSpec(memory_space=pltpu.SMEM),
            pl.BlockSpec(memory_space=pltpu.VMEM),
        ],
        out_specs=(
            pl.BlockSpec(memory_space=pltpu.VMEM),
            pl.BlockSpec(memory_space=pltpu.SMEM),
        ),
        scratch_shapes=[pltpu.VMEM((4, BLOCKS, 2 * BLOCKS), jnp.float32)],
        compiler_params=pltpu.CompilerParams(vmem_limit_bytes=16 * 1024 * 1024),
        name="power",
    )(place.reshape(1), sums)


def shards(snapshots, tail):
    points = snapshots.shape[0]
    space = lax.axis_index("space")
    freq = lax.axis_index("freq")
    each = points // GROUPS
    table = build_table()
    scale = 1.0 / (points * GROUPS * (0.375 * NFFT))
    raw = lax.all_to_all(snapshots.reshape(GROUPS, each, NFFT), "freq", 0, 0)
    own_tail = lax.dynamic_slice_in_dim(tail, freq * each, each, 0)
    core = space % 2
    chip = space // 2
    factor = jnp.exp2(chip.astype(jnp.float32) / CHIPS)
    own, other = gram_call(core, factor, raw, own_tail, table)
    other = lax.ppermute(other, "space", [(s, s ^ 1) for s in range(GROUPS)])
    sums = own * factor + other.astype(jnp.float32)
    undo = jnp.asarray(np.exp2(-np.arange(CHIPS) / CHIPS), jnp.float32)[:, None, None]
    parts = lax.all_to_all(
        sums.astype(jnp.bfloat16),
        "space",
        0,
        0,
        axis_index_groups=[[2 * i + c for i in range(CHIPS)] for c in range(2)],
    )
    mine = jnp.sum(parts.astype(jnp.float32) * undo, 0).reshape(GROUPS, 4, 2 * BLOCKS)
    mine = jnp.sum(lax.all_to_all(mine, "freq", 0, 0), 0)
    whole = lax.all_to_all(jnp.broadcast_to(mine[None], (GROUPS,) + mine.shape), "space", 0, 0)
    return power_call(space, scale, whole)


def solution(mesh):
    in_specs = (P("space", "freq"), P("space", None))
    out_specs = (P("freq", None, "space", None), P("freq"))
    return jax.shard_map(shards, mesh=mesh, in_specs=in_specs, out_specs=out_specs, check_vma=False)
```

```python
import functools
import math

import jax
import jax.numpy as jnp
import numpy as np
from jax import lax
from jax.experimental import pallas as pl
from jax.experimental.pallas import tpu as pltpu
from jax.sharding import PartitionSpec as P

NFFT = 256
HALF = NFFT // 2
POWER = 4
BLOCKS = 64
FREQS = 128
PITCH = 2 * FREQS + 8
GROUPS = 32
CHIPS = GROUPS // 2
ORDER = [(r % 4) * 8 + r // 4 for r in range(GROUPS)]
RANK = [ORDER.index(z) for z in range(GROUPS)]
NT = (((1,), (1,)), ((), ()))


def build_table():
    steps = jnp.arange(NFFT, dtype=jnp.int32)
    freqs = jnp.arange(FREQS, dtype=jnp.int32)
    window = 0.5 - 0.5 * jnp.cos(2.0 * math.pi * steps.astype(jnp.float32) / NFFT)
    phase = 2.0 * math.pi * (freqs[:, None] * steps[None, :] % NFFT).astype(jnp.float32) / NFFT
    table = jnp.concatenate(
        [window[None, :] * jnp.cos(phase), -window[None, :] * jnp.sin(phase)], 0
    )
    return table.astype(jnp.bfloat16)


def gram_kernel(unroll, core_ref, factor_ref, raw_ref, tail_ref, table_ref, own_ref, other_ref, coef_ref, held_ref):
    def put(block, rows):
        coef = lax.dot_general(table_ref[...], rows, NT, preferred_element_type=jnp.float32)
        coef_ref[pl.ds(block * PITCH, 2 * FREQS), :] = coef

    for z in range(GROUPS):
        rows = raw_ref[RANK[z]]
        after = tail_ref[...] if z == GROUPS - 1 else raw_ref[RANK[z + 1]][:, :HALF]
        put(2 * z, rows)
        put(2 * z + 1, jnp.concatenate([rows[:, HALF:], after], 1))

    row = lax.broadcasted_iota(jnp.int32, (BLOCKS, 2 * BLOCKS), 0)
    lane = lax.broadcasted_iota(jnp.int32, (BLOCKS, 2 * BLOCKS), 1)
    first = ((lane < BLOCKS) & (row <= lane)) | ((lane >= BLOCKS) & (row > lane - BLOCKS))

    def product(f, swap):
        real = coef_ref[pl.ds(f, BLOCKS, stride=PITCH), :].astype(jnp.bfloat16)
        imag = coef_ref[pl.ds(FREQS + f, BLOCKS, stride=PITCH), :].astype(jnp.bfloat16)
        left = jnp.concatenate([real, imag], 1)
        turned = jnp.concatenate([imag, -real], 1)
        right = jnp.concatenate([turned, left] if swap else [left, turned], 0)
        return lax.dot_general(left, right, NT, preferred_element_type=jnp.float32)

    def packed(f):
        return jnp.where(first, product(f, False), product(f + 1, True))

    core = core_ref[0]

    def half(target_ref, core):
        def gram(step, carry):
            base = 8 * step
            upper = packed(base + 2 * core)
            lower = packed(base + 4 + 2 * core)
            start = pl.multiple_of(base, 8)
            for chip in range(CHIPS):
                part = slice(4 * chip, 4 * chip + 4)
                target_ref[chip, pl.ds(start, 8), :] = jnp.concatenate(
                    [upper[part], lower[part]], 0
                )
            return carry

        lax.fori_loop(0, FREQS // 8, gram, 0, unroll=unroll)

    half(held_ref, 1 - core)
    other_ref[...] = (held_ref[...] * factor_ref[0]).astype(jnp.bfloat16)
    half(own_ref, core)


def gram_call(core, factor, raw, tail, table, unroll=16):
    points = raw.shape[1]
    shape = (CHIPS, FREQS, 2 * BLOCKS)
    return pl.pallas_call(
        functools.partial(gram_kernel, unroll),
        out_shape=(
            jax.ShapeDtypeStruct(shape, jnp.float32),
            jax.ShapeDtypeStruct(shape, jnp.bfloat16),
        ),
        in_specs=[
            pl.BlockSpec(memory_space=pltpu.SMEM),
            pl.BlockSpec(memory_space=pltpu.SMEM),
            pl.BlockSpec(memory_space=pltpu.VMEM),
            pl.BlockSpec(memory_space=pltpu.VMEM),
            pl.BlockSpec(memory_space=pltpu.VMEM),
        ],
        out_specs=(
            pl.BlockSpec(memory_space=pltpu.VMEM),
            pl.BlockSpec(memory_space=pltpu.VMEM),
        ),
        scratch_shapes=[
            pltpu.VMEM((BLOCKS * PITCH, points), jnp.float32),
            pltpu.VMEM(shape, jnp.float32),
        ],
        compiler_params=pltpu.CompilerParams(vmem_limit_bytes=20 * 1024 * 1024),
        name="gram",
    )(core.reshape(1), factor.reshape(1), raw, tail, table)


def power_kernel(scale, place_ref, sums_ref, rows_ref, spectrum_ref, matrix_ref):
    row = lax.broadcasted_iota(jnp.int32, (BLOCKS, BLOCKS), 0)
    column = lax.broadcasted_iota(jnp.int32, (BLOCKS, BLOCKS), 1)
    matrices = []
    for core in range(2):
        held = jnp.concatenate([sums_ref[2 * c + core] for c in range(CHIPS)], 0) * scale
        left, right = (held[:, :BLOCKS], held[:, BLOCKS:])
        left_t, right_t = (left.T, right.T)
        real_even = jnp.where(row <= column, left, left_t)
        real_odd = jnp.where(row <= column, right, right_t)
        zero = jnp.zeros_like(left)
        imag_odd = jnp.where(row > column, left, jnp.where(row < column, -left_t, zero))
        imag_even = jnp.where(row > column, right, jnp.where(row < column, -right_t, zero))
        matrices.append(jnp.concatenate([real_even, imag_even], 1))
        matrices.append(jnp.concatenate([real_odd, imag_odd], 1))
    matrix = jnp.stack(matrices, 0)
    matrix_ref[...] = matrix
    place = place_ref[0]
    for k in range(2):
        line = matrix_ref[:, pl.ds(2 * place + k, 1), :]
        rows_ref[:, 0, k : k + 1, :] = line[:, :, :BLOCKS]
        rows_ref[:, 1, k : k + 1, :] = line[:, :, BLOCKS:]

    low = lax.broadcasted_iota(jnp.int32, (4, 1, 2 * BLOCKS), 2) < BLOCKS
    count = 2.0 * BLOCKS

    def turn(v):
        return jnp.concatenate([v[:, :, BLOCKS:], v[:, :, :BLOCKS]], 2)

    def from_columns(v_real, v_imag):
        a = jnp.sum(matrix * v_real, axis=1, keepdims=True)
        b = jnp.sum(matrix * v_imag, axis=1, keepdims=True)
        return jnp.where(low, a, -a) + turn(b)

    def from_rows(v):
        u_real = jnp.sum(matrix * jnp.where(low, v, -v), axis=2, keepdims=True)
        u_imag = jnp.sum(matrix * turn(v), axis=2, keepdims=True)
        return (u_real, u_imag)

    def scaled_columns(u_real, u_imag):
        m = jnp.sum(u_real * u_real + u_imag * u_imag, axis=1, keepdims=True) / count
        norm = jnp.sqrt(m + 1e-06)
        return (u_real / norm, u_imag / norm)

    def scaled_rows(u):
        return u / jnp.sqrt(jnp.sum(u * u, axis=2, keepdims=True) / count + 1e-06)

    v = jnp.where(low, jnp.ones((4, 1, 2 * BLOCKS), jnp.float32), 0.0)
    for step in range(POWER // 2):
        v = scaled_rows(from_columns(*scaled_columns(*from_rows(v))))
    u_real, u_imag = from_rows(v)
    lane = lax.broadcasted_iota(jnp.int32, (4, BLOCKS, 2 * BLOCKS), 2)
    line = lax.broadcasted_iota(jnp.int32, (4, BLOCKS, 2 * BLOCKS), 1)
    v_real = jnp.sum(jnp.where(lane == line, v, 0.0), axis=2, keepdims=True)
    v_imag = jnp.sum(jnp.where(lane == line + BLOCKS, v, 0.0), axis=2, keepdims=True)
    top = jnp.sum(v_real * u_real + v_imag * u_imag, axis=1, keepdims=True) / count
    below = jnp.sum(v_real * v_real + v_imag * v_imag, axis=1, keepdims=True) / count
    ratio = top / (below + 1e-06)
    for f in range(4):
        spectrum_ref[f] = ratio[f, 0, 0]


def power_call(place, scale, sums):
    return pl.pallas_call(
        functools.partial(power_kernel, scale),
        out_shape=(
            jax.ShapeDtypeStruct((4, 2, 2, BLOCKS), jnp.float32),
            jax.ShapeDtypeStruct((4,), jnp.float32),
        ),
        in_specs=[
            pl.BlockSpec(memory_space=pltpu.SMEM),
            pl.BlockSpec(memory_space=pltpu.VMEM),
        ],
        out_specs=(
            pl.BlockSpec(memory_space=pltpu.VMEM),
            pl.BlockSpec(memory_space=pltpu.SMEM),
        ),
        scratch_shapes=[pltpu.VMEM((4, BLOCKS, 2 * BLOCKS), jnp.float32)],
        compiler_params=pltpu.CompilerParams(vmem_limit_bytes=16 * 1024 * 1024),
        name="power",
    )(place.reshape(1), sums)


def shards(snapshots, tail):
    points = snapshots.shape[0]
    space = lax.axis_index("space")
    freq = lax.axis_index("freq")
    each = points // GROUPS
    table = build_table()
    scale = 1.0 / (points * GROUPS * (0.375 * NFFT))
    raw = lax.all_to_all(
        snapshots.reshape(GROUPS, each, NFFT), "freq", 0, 0, axis_index_groups=[ORDER]
    )
    rank = (freq % 8) * 4 + freq // 8
    own_tail = lax.dynamic_slice_in_dim(tail, rank * each, each, 0)
    core = space % 2
    chip = space // 2
    factor = jnp.exp2(chip.astype(jnp.float32) / CHIPS)
    own, other = gram_call(core, factor, raw, own_tail, table)
    other = lax.ppermute(other, "space", [(s, s ^ 1) for s in range(GROUPS)])
    sums = own * factor + other.astype(jnp.float32)
    undo = jnp.asarray(np.exp2(-np.arange(CHIPS) / CHIPS), jnp.float32)[:, None, None]
    parts = lax.all_to_all(
        sums.astype(jnp.bfloat16),
        "space",
        0,
        0,
        axis_index_groups=[[2 * i + c for i in range(CHIPS)] for c in range(2)],
    )
    mine = jnp.sum(parts.astype(jnp.float32) * undo, 0).reshape(GROUPS, 4, 2 * BLOCKS)
    mine = jnp.sum(lax.all_to_all(mine, "freq", 0, 0), 0)
    whole = lax.all_to_all(jnp.broadcast_to(mine[None], (GROUPS,) + mine.shape), "space", 0, 0)
    return power_call(space, scale, whole)


def solution(mesh):
    in_specs = (P("space", "freq"), P("space", None))
    out_specs = (P("freq", None, "space", None), P("freq"))
    return jax.shard_map(shards, mesh=mesh, in_specs=in_specs, out_specs=out_specs, check_vma=False)
```
